32 devices in a mesh: pair: 8 (over z, x), slab: 4 (over y, core).
Axes of the slice: x: 2, y: 2, z: 4, core: 2. Of those that a mesh axis runs over, the one named last changes fastest.
Arguments:
- amplitudes: bfloat16 [8, 4096, 512], P(None, 'slab', 'pair'), may hold values from -6 to 6
- integrals: bfloat16 [64, 4096, 512], P('pair', 'slab'), may hold values from -0.09375 to 0.09375
- other_terms: bfloat16 [64, 512, 512], P(None, ('pair', 'slab')), may hold values from -6 to 6
- occ_energy: float32 [8, 512], P(None, ('pair', 'slab')), may hold values from -3 to -1
- vir_energy: float32 [64, 512], replicated, may hold values from 1 to 3
- block_tiles: int32 [64], replicated, may hold values from 1 to 4, as said below
- block_irrep: int32 [64], replicated, may hold values from 0 to 7
- block_order: int32 [64], replicated, may hold values from 0 to 63, as said below
Outputs:
- increment: bfloat16 [64, 512, 512], P(None, ('pair', 'slab'))
The draws below stay inside these ranges and needn't reach their ends.
Inputs may be any that keep to these rules, and one draw needn't show every extreme that they name: `block_order`: A permutation of the blocks; it lists all blocks of irrep 0 first, then those of irrep 1, and so on. `block_tiles`: some block has 4 tiles. The blocks of one irrep, which changes from draw to draw, have more than half of 4 tiles; all others have at most half of 4.
All inputs are finite; a program needn't handle non-finite values.
Results may differ from the reference program's by a relative error of at most 0.001.
Values may be sent and summed in bfloat16 or wider, within the bound.
A program may use at most 128 MiB of HBM per device.

```python
import jax
import jax.numpy as jnp
from jax import lax

NIRR = 8
OPG = 512
MAXT = 4
WMAX = 512
NBLK = 64
CD = 4096


def sector_layout(key):
    key_label, key_widest, key_wide, key_narrow, key_shuffle = jax.random.split(key, 5)
    labels = jax.random.randint(key_label, (NBLK,), 0, NIRR).astype(jnp.int32)
    widest = jax.random.randint(key_widest, (), 0, NBLK)
    wide_label = labels[widest]
    half_tiles = MAXT // 2
    wide_tiles = jax.random.randint(key_wide, (NBLK,), half_tiles + 1, MAXT + 1)
    narrow_tiles = jax.random.randint(key_narrow, (NBLK,), 1, half_tiles + 1)
    tiles = jnp.where(labels == wide_label, wide_tiles, narrow_tiles).at[widest].set(MAXT).astype(jnp.int32)
    scores = labels * NBLK + jax.random.permutation(key_shuffle, NBLK).astype(jnp.int32)
    ordering = jnp.argsort(scores, stable=True).astype(jnp.int32)
    return (labels, tiles, ordering)


def draw_block_tiles(key, part):
    return sector_layout(key)[1]


def draw_block_irrep(key, part):
    return sector_layout(key)[0]


def draw_block_order(key, part):
    return sector_layout(key)[2]


def steps_of(key, extent, shards, smallest, largest):
    level, own = 1.0, jax.random.fold_in(key, 6)
    for position, parts in shards:
        heights = jnp.exp(jax.random.uniform(jax.random.fold_in(own, position), (parts,), jnp.float32, smallest / len(shards), largest / len(shards)))
        level = level * jnp.repeat(heights, extent[position] // parts).reshape([-1 if axis == position else 1 for axis in range(len(extent))])
    return level


def normal_values(stream_key, dims, deviation, bound, cuts=(), held_as=jnp.bfloat16):
    drawn = deviation * jax.random.normal(stream_key, dims, jnp.float32)
    if cuts:
        drawn = drawn * steps_of(stream_key, dims, cuts, -0.22, 0.18)
    return jnp.clip(drawn, -bound, bound).astype(held_as)


def setup_inputs(seed: int = 0) -> dict:
    key_of = jax.random.split(jax.random.key(seed), 9)
    amplitudes = normal_values(key_of[0], (NIRR, CD, OPG), 1.0, 6.0, ((1, 4), (2, 8)))
    integrals = normal_values(key_of[1], (NBLK, CD, WMAX), CD ** -0.5, 0.09375, ((0, 8), (1, 4)))
    other_terms = normal_values(key_of[2], (NBLK, OPG, WMAX), 1.0, 6.0, ((1, 32),))
    occ_energy = jnp.clip(-3.0 + 2.0 * jax.random.uniform(key_of[3], (NIRR, OPG), jnp.float32) ** steps_of(key_of[3], (NIRR, OPG), ((1, 32),), -0.2, 0.2), -3.0, -1.0)
    vir_energy = jnp.clip(jax.random.uniform(key_of[4], (NBLK, WMAX), jnp.float32, 1.0, 3.0), 1.0, 3.0)
    block_tiles = draw_block_tiles(jax.random.fold_in(key_of[8], 71), 0)
    block_irrep = draw_block_irrep(jax.random.fold_in(key_of[8], 71), 0)
    block_order = draw_block_order(jax.random.fold_in(key_of[8], 71), 0)
    return dict(amplitudes=amplitudes, integrals=integrals, other_terms=other_terms, occ_energy=occ_energy, vir_energy=vir_energy, block_tiles=block_tiles, block_irrep=block_irrep, block_order=block_order)


def reference(amplitudes, integrals, other_terms, occ_energy, vir_energy, block_tiles, block_irrep, block_order):
    inverse = jnp.argsort(block_order).astype(jnp.int32)
    columns = jnp.arange(WMAX, dtype=jnp.int32)

    def one_block(items):
        label, slot, tiles, extra, vir_row = items
        amp_plane = lax.dynamic_index_in_dim(amplitudes, label, 0, keepdims=False)
        plane = lax.dynamic_index_in_dim(integrals, slot, 0, keepdims=False)
        ladder = jnp.dot(amp_plane.T, plane, preferred_element_type=jnp.float32)
        occ_row = lax.dynamic_index_in_dim(occ_energy, label, 0, keepdims=False)
        divisor = vir_row[None, :] - occ_row[:, None]
        live_mask = columns[None, :] < 128 * tiles
        value = (ladder + extra.astype(jnp.float32)) / divisor
        return jnp.where(live_mask, value, jnp.zeros_like(value)).astype(jnp.bfloat16)

    return lax.map(one_block, (block_irrep, inverse, block_tiles, other_terms, vir_energy))
```

```python
import functools

import jax
import jax.numpy as jnp
from jax import lax
from jax.sharding import PartitionSpec as P

from jax.experimental import pallas as pl
from jax.experimental.pallas import tpu as pltpu

tile_width = 128
quant_top = 32766.0
quant_floor = 1e-33
window = 3


def gathered_path(
    amplitudes,
    integrals,
    other_terms,
    occ_energy,
    vir_energy,
    block_tiles,
    block_irrep,
    block_order,
):
    pair_count = lax.axis_size("pair")
    slab_count = lax.axis_size("slab")
    slot_count, cd_local, width_max = integrals.shape
    first_slot = lax.axis_index("pair") * slot_count
    my_blocks = lax.dynamic_slice_in_dim(block_order, first_slot, slot_count)
    my_labels = jnp.take(block_irrep, my_blocks)
    chosen = jnp.take(lax.all_gather(amplitudes, "pair", axis=2, tiled=True), my_labels, axis=0)
    ladder = jnp.einsum("bkr,bkw->brw", chosen, integrals, preferred_element_type=jnp.float32)
    row_share = ladder.shape[1] // (pair_count * slab_count)
    ladder = ladder.reshape(slot_count, pair_count, slab_count, row_share, width_max)
    total = lax.psum(ladder, "slab")
    my_share = lax.dynamic_slice_in_dim(total, lax.axis_index("slab"), 1, 2)
    returned = lax.all_to_all(my_share, "pair", split_axis=1, concat_axis=0, tiled=True)
    returned = returned.reshape(pair_count * slot_count, row_share, width_max)
    inverse = jnp.argsort(block_order)
    ordered = jnp.take(returned, inverse, axis=0)
    label_count = occ_energy.shape[0]
    one_hot = (block_irrep[:, None] == jnp.arange(label_count, dtype=jnp.int32)[None, :]).astype(
        jnp.float32
    )
    occ_rows = jnp.dot(one_hot, occ_energy, precision=lax.Precision.HIGHEST)
    divisor = vir_energy[:, None, :] - occ_rows[:, :, None]
    columns = jnp.arange(width_max, dtype=jnp.int32)
    live_mask = columns[None, None, :] < (tile_width * block_tiles)[:, None, None]
    value = (ordered + other_terms.astype(jnp.float32)) / divisor
    return jnp.where(live_mask, value, jnp.zeros_like(value)).astype(jnp.bfloat16)


def quantize(value):
    top = jnp.maximum(jnp.max(jnp.abs(value), axis=0, keepdims=True), quant_floor)
    code = jnp.round(value * (quant_top / top)).astype(jnp.int32).astype(jnp.int16)
    return code, top * (1.0 / quant_top)


def widen(code, scale):
    return code.astype(jnp.int32).astype(jnp.float32) * scale


def ladder_kernel(
    pair_count,
    slab_count,
    capacity,
    needed_ref,
    rank_ref,
    inverse_ref,
    label_ref,
    tiles_ref,
    amplitudes_ref,
    integrals_ref,
    other_ref,
    occ_ref,
    vir_ref,
    out_ref,
    slab_data,
    staged,
    got,
    product,
    own,
    part_out,
    part_out_scale,
    part_in,
    part_in_scale,
    back_out,
    back_out_scale,
    back_in,
    back_in_scale,
    slab_sem,
    amp_sems,
    part_sems,
    part_scale_sems,
    back_sems,
    back_scale_sems,
):
    slots = integrals_ref.shape[0]
    share = own.shape[2]
    width = own.shape[3]
    block_count = out_ref.shape[0]
    p = lax.axis_index("pair")
    s = lax.axis_index("slab")

    def load(j):
        return pltpu.make_async_copy(integrals_ref.at[j], slab_data.at[j], slab_sem.at[j])

    for j in range(slots):
        load(j).start()

    barrier = pltpu.get_barrier_semaphore()
    for d in range(1, pair_count):
        pl.semaphore_signal(barrier, inc=1, device_id=(lax.rem(p + d, pair_count), s), device_id_type=pl.DeviceIdType.MESH)
    for e in range(1, slab_count):
        pl.semaphore_signal(barrier, inc=1, device_id=(p, lax.rem(s + e, slab_count)), device_id_type=pl.DeviceIdType.MESH)
    pl.semaphore_wait(barrier, pair_count + slab_count - 2)

    def distance(i):
        return i // 2 + lax.rem(i, 2) * (pair_count // 2)

    def ahead(i):
        return lax.rem(p + distance(i), pair_count)

    def behind(i):
        return lax.rem(p + pair_count - distance(i), pair_count)

    def remote(source, target, sems, at, device):
        return pltpu.make_async_remote_copy(
            src_ref=source,
            dst_ref=target,
            send_sem=sems.at[(0,) + at],
            recv_sem=sems.at[(1,) + at],
            device_id=device,
            device_id_type=pl.DeviceIdType.MESH,
        )

    def amp_copy(i):
        return remote(staged.at[i], got.at[i], amp_sems, (i,), (ahead(i), s))

    def part_copies(i, e):
        device = (p, lax.rem(s + e, slab_count))
        return (
            remote(part_out.at[i, e - 1], part_in.at[i, e - 1], part_sems, (i, e - 1), device),
            remote(part_out_scale.at[i, e - 1], part_in_scale.at[i, e - 1], part_scale_sems, (i, e - 1), device),
        )

    mine = pl.ds(pl.multiple_of(p * slots, slots), slots)

    def back_copies(i):
        device = (behind(i), s)
        return (
            remote(back_out.at[i], back_in.at[mine], back_sems, (i,), device),
            remote(back_out_scale.at[i], back_in_scale.at[mine], back_scale_sems, (i,), device),
        )

    def send_amplitudes(i):
        for c in range(capacity):
            staged[i, c] = amplitudes_ref[needed_ref[ahead(i), c]]
        amp_copy(i).start()

    def multiply(i):
        @pl.loop(0, slots)
        def _(j):
            rank = rank_ref[p, j]
            chosen = got[i, 0]
            for c in range(1, capacity):
                chosen = jnp.where(rank == c, got[i, c], chosen)
            product[...] = jnp.dot(chosen, slab_data[j], preferred_element_type=jnp.float32)
            for e in range(slab_count):
                start = pl.multiple_of(lax.rem(s + e, slab_count) * share, share)
                rows = product[pl.ds(start, share), :]
                if e == 0:
                    own[i, j] = rows
                else:
                    code, scale = quantize(rows)
                    part_out[i, e - 1, j] = code
                    part_out_scale[i, e - 1, pl.ds(j, 1), :] = scale

        for e in range(1, slab_count):
            for copy in part_copies(i, e):
                copy.start()

    def add_up(i, codes, scales, first):
        for e in range(1, slab_count):
            for copy in part_copies(i, e):
                copy.wait_recv()

        @pl.loop(0, slots)
        def _(j):
            total = own[i, j]
            for e in range(1, slab_count):
                total += widen(part_in[i, e - 1, j], part_in_scale[i, e - 1, pl.ds(j, 1), :])
            code, scale = quantize(total)
            codes[first + j] = code
            scales[pl.ds(first + j, 1), :] = scale

    def return_rows(i):
        add_up(i, back_out.at[i], back_out_scale.at[i], 0)
        for copy in back_copies(i):
            copy.start()

    for i in range(1, min(window, pair_count - 1) + 1):
        send_amplitudes(i)
    for c in range(capacity):
        got[0, c] = amplitudes_ref[needed_ref[p, c]]
    for j in range(slots):
        load(j).wait()
    multiply(0)

    @pl.loop(1, pair_count)
    def _(i):
        amp_copy(i).wait_recv()

        @pl.when(i + window < pair_count)
        def _():
            send_amplitudes(i + window)

        multiply(i)

        @pl.when(i == 1)
        def _():
            add_up(0, back_in, back_in_scale, p * slots)

        @pl.when(i > 1)
        def _():
            return_rows(i - 1)

    return_rows(pair_count - 1)

    @pl.loop(1, pair_count)
    def _(i):
        for copy in back_copies(i):
            copy.wait_recv()

    columns = lax.broadcasted_iota(jnp.int32, (share, width), 1)

    @pl.loop(0, block_count)
    def _(b):
        k = inverse_ref[b]
        ladder = widen(back_in[k], back_in_scale[pl.ds(k, 1), :])
        occ = jnp.concatenate([occ_ref[label_ref[b]]] * (width // tile_width), axis=1)
        divisor = vir_ref[pl.ds(b, 1), :] - occ
        value = (ladder + other_ref[b].astype(jnp.float32)) / divisor
        live = columns < tile_width * tiles_ref[b]
        out_ref[b] = jnp.where(live, value, jnp.zeros_like(value)).astype(out_ref.dtype)

    @pl.loop(1, pair_count)
    def _(i):
        amp_copy(i).wait_send()
        for copy in back_copies(i):
            copy.wait_send()

    @pl.loop(0, pair_count)
    def _(i):
        for e in range(1, slab_count):
            for copy in part_copies(i, e):
                copy.wait_send()


def kernel_path(capacity, amplitudes, integrals, other_terms, occ_energy, vir_energy, block_tiles, block_irrep, inverse, needed, rank):
    n = lax.axis_size("pair")
    m = lax.axis_size("slab")
    slots, depth, width = integrals.shape
    rows = amplitudes.shape[2]
    share = rows // m
    blocks = n * slots
    turned = jnp.swapaxes(amplitudes, 1, 2)
    occ_wide = jnp.broadcast_to(occ_energy[:, :, None], occ_energy.shape + (tile_width,))
    smem = pl.BlockSpec(memory_space=pltpu.SMEM)
    vmem = pl.BlockSpec(memory_space=pltpu.VMEM)
    f32, i16, bf16 = jnp.float32, jnp.int16, jnp.bfloat16
    return pl.pallas_call(
        functools.partial(ladder_kernel, n, m, capacity),
        out_shape=jax.ShapeDtypeStruct(other_terms.shape, bf16),
        in_specs=[smem] * 5 + [vmem, pl.BlockSpec(memory_space=pl.ANY)] + [vmem] * 3,
        out_specs=vmem,
        scratch_shapes=[
            pltpu.VMEM((slots, depth, width), bf16),
            pltpu.VMEM((n, capacity, rows, depth), bf16),
            pltpu.VMEM((n, capacity, rows, depth), bf16),
            pltpu.VMEM((rows, width), f32),
            pltpu.VMEM((n, slots, share, width), f32),
            pltpu.VMEM((n, m - 1, slots, share, width), i16),
            pltpu.VMEM((n, m - 1, slots, width), f32),
            pltpu.VMEM((n, m - 1, slots, share, width), i16),
            pltpu.VMEM((n, m - 1, slots, width), f32),
            pltpu.VMEM((n, slots, share, width), i16),
            pltpu.VMEM((n, slots, width), f32),
            pltpu.VMEM((blocks, share, width), i16),
            pltpu.VMEM((blocks, width), f32),
            pltpu.SemaphoreType.DMA((slots,)),
            pltpu.SemaphoreType.DMA((2, n)),
            pltpu.SemaphoreType.DMA((2, n, m - 1)),
            pltpu.SemaphoreType.DMA((2, n, m - 1)),
            pltpu.SemaphoreType.DMA((2, n)),
            pltpu.SemaphoreType.DMA((2, n)),
        ],
        compiler_params=pltpu.CompilerParams(
            collective_id=capacity, has_side_effects=True, vmem_limit_bytes=50 * 1024 * 1024
        ),
        cost_estimate=pl.CostEstimate(
            flops=2 * slots * n * rows * depth * width, bytes_accessed=2 * slots * depth * width, transcendentals=0
        ),
    )(needed, rank, inverse, block_irrep, block_tiles, turned, integrals, other_terms, occ_wide, vir_energy)


def shards(
    amplitudes,
    integrals,
    other_terms,
    occ_energy,
    vir_energy,
    block_tiles,
    block_irrep,
    block_order,
):
    whole = (amplitudes, integrals, other_terms, occ_energy, vir_energy, block_tiles, block_irrep, block_order)
    n = lax.axis_size("pair")
    slots = integrals.shape[0]
    share = amplitudes.shape[2] // lax.axis_size("slab")
    if share % 16 or slots % 8 or n % 2 or n > 16:
        return gathered_path(*whole)
    numbers = jnp.arange(n * slots, dtype=jnp.int32)
    inverse = jnp.sum(jnp.where(block_order[None, :] == numbers[:, None], numbers[None, :], 0), axis=1)
    labels = jnp.sum(jnp.where(block_order[:, None] == numbers[None, :], block_irrep[None, :], 0), axis=1)
    labels = labels.reshape(n, slots)
    changed = (labels[:, 1:] != labels[:, :-1]).astype(jnp.int32)
    order = jnp.arange(slots, dtype=jnp.int32)
    changed = jnp.pad(changed, ((0, 0), (1, 0)))
    rank = jnp.sum(jnp.where(order[None, None, :] <= order[None, :, None], changed[:, None, :], 0), axis=2)
    most = jnp.max(rank) + 1

    def run(capacity):
        places = jnp.arange(capacity, dtype=jnp.int32)
        needed = jnp.max(jnp.where(rank[:, :, None] == places, labels[:, :, None], 0), axis=1)
        return lambda: kernel_path(
            capacity, amplitudes, integrals, other_terms, occ_energy, vir_energy, block_tiles, block_irrep, inverse, needed, rank
        )

    choice = jnp.clip(most - 2, 0, 3)
    return lax.switch(choice, [run(2), run(3), run(4), lambda: gathered_path(*whole)])


def solution(mesh):
    return jax.shard_map(
        shards,
        mesh=mesh,
        in_specs=(
            P(None, "slab", "pair"),
            P("pair", "slab", None),
            P(None, ("pair", "slab"), None),
            P(None, ("pair", "slab")),
            P(),
            P(),
            P(),
            P(),
        ),
        out_specs=P(None, ("pair", "slab"), None),
        check_vma=False,
    )
```

```python
import functools

import jax
import jax.numpy as jnp
from jax import lax
from jax.sharding import PartitionSpec as P

from jax.experimental import pallas as pl
from jax.experimental.pallas import tpu as pltpu

tile_width = 128
quant_top = 32766.0
quant_floor = 1e-33
window = 2


def gathered_path(
    amplitudes,
    integrals,
    other_terms,
    occ_energy,
    vir_energy,
    block_tiles,
    block_irrep,
    block_order,
):
    pair_count = lax.axis_size("pair")
    slab_count = lax.axis_size("slab")
    slot_count, cd_local, width_max = integrals.shape
    first_slot = lax.axis_index("pair") * slot_count
    my_blocks = lax.dynamic_slice_in_dim(block_order, first_slot, slot_count)
    my_labels = jnp.take(block_irrep, my_blocks)
    chosen = jnp.take(lax.all_gather(amplitudes, "pair", axis=2, tiled=True), my_labels, axis=0)
    ladder = jnp.einsum("bkr,bkw->brw", chosen, integrals, preferred_element_type=jnp.float32)
    row_share = ladder.shape[1] // (pair_count * slab_count)
    ladder = ladder.reshape(slot_count, pair_count, slab_count, row_share, width_max)
    total = lax.psum(ladder, "slab")
    my_share = lax.dynamic_slice_in_dim(total, lax.axis_index("slab"), 1, 2)
    returned = lax.all_to_all(my_share, "pair", split_axis=1, concat_axis=0, tiled=True)
    returned = returned.reshape(pair_count * slot_count, row_share, width_max)
    inverse = jnp.argsort(block_order)
    ordered = jnp.take(returned, inverse, axis=0)
    label_count = occ_energy.shape[0]
    one_hot = (block_irrep[:, None] == jnp.arange(label_count, dtype=jnp.int32)[None, :]).astype(
        jnp.float32
    )
    occ_rows = jnp.dot(one_hot, occ_energy, precision=lax.Precision.HIGHEST)
    divisor = vir_energy[:, None, :] - occ_rows[:, :, None]
    columns = jnp.arange(width_max, dtype=jnp.int32)
    live_mask = columns[None, None, :] < (tile_width * block_tiles)[:, None, None]
    value = (ordered + other_terms.astype(jnp.float32)) / divisor
    return jnp.where(live_mask, value, jnp.zeros_like(value)).astype(jnp.bfloat16)


def quantize(value):
    top = jnp.maximum(jnp.max(jnp.abs(value), axis=0, keepdims=True), quant_floor)
    code = jnp.round(value * (quant_top / top)).astype(jnp.int32).astype(jnp.int16)
    return code, top * (1.0 / quant_top)


def widen(code, scale):
    return code.astype(jnp.int32).astype(jnp.float32) * scale


def ladder_kernel(
    pair_count,
    slab_count,
    capacity,
    needed_ref,
    rank_ref,
    inverse_ref,
    label_ref,
    tiles_ref,
    amplitudes_ref,
    integrals_ref,
    other_ref,
    occ_ref,
    vir_ref,
    out_ref,
    slab_data,
    staged,
    got,
    product,
    own,
    part_out,
    part_out_scale,
    part_in,
    part_in_scale,
    back_out,
    back_out_scale,
    back_in,
    back_in_scale,
    slab_sem,
    amp_sems,
    part_sems,
    part_scale_sems,
    back_sems,
    back_scale_sems,
):
    slots = integrals_ref.shape[0]
    share = own.shape[2]
    width = own.shape[3]
    block_count = out_ref.shape[0]
    p = lax.axis_index("pair")
    s = lax.axis_index("slab")

    def load(j):
        return pltpu.make_async_copy(integrals_ref.at[j], slab_data.at[j], slab_sem.at[j])

    for j in range(slots):
        load(j).start()

    barrier = pltpu.get_barrier_semaphore()
    for d in range(1, pair_count):
        pl.semaphore_signal(barrier, inc=1, device_id=(lax.rem(p + d, pair_count), s), device_id_type=pl.DeviceIdType.MESH)
    for e in range(1, slab_count):
        pl.semaphore_signal(barrier, inc=1, device_id=(p, lax.rem(s + e, slab_count)), device_id_type=pl.DeviceIdType.MESH)
    pl.semaphore_wait(barrier, pair_count + slab_count - 2)

    planes = pair_count // 2
    plane, side = p // 2, lax.rem(p, 2)
    partner = 2 * plane + 1 - side

    def distance(k):
        return k // 2 + lax.rem(k, 2) * (planes // 2)

    def ahead(k):
        return 2 * lax.rem(plane + distance(k), planes) + side

    def behind(i):
        return 2 * lax.rem(plane + planes - distance(i // 2), planes) + lax.rem(side + lax.rem(i, 2), 2)

    def remote(source, target, sems, at, device):
        return pltpu.make_async_remote_copy(
            src_ref=source,
            dst_ref=target,
            send_sem=sems.at[(0,) + at],
            recv_sem=sems.at[(1,) + at],
            device_id=device,
            device_id_type=pl.DeviceIdType.MESH,
        )

    def amp_copy(k):
        return remote(staged.at[k], got.at[2 * k], amp_sems, (2 * k,), (ahead(k), s))

    def relay_copy(k):
        return remote(got.at[2 * k], got.at[2 * k + 1], amp_sems, (2 * k + 1,), (partner, s))

    def part_copies(i, e):
        device = (p, lax.rem(s + e, slab_count))
        return (
            remote(part_out.at[i, e - 1], part_in.at[i, e - 1], part_sems, (i, e - 1), device),
            remote(part_out_scale.at[i, e - 1], part_in_scale.at[i, e - 1], part_scale_sems, (i, e - 1), device),
        )

    mine = pl.ds(pl.multiple_of(p * slots, slots), slots)

    def back_copies(i):
        device = (behind(i), s)
        return (
            remote(back_out.at[i], back_in.at[mine], back_sems, (i,), device),
            remote(back_out_scale.at[i], back_in_scale.at[mine], back_scale_sems, (i,), device),
        )

    def send_amplitudes(k):
        for c in range(capacity):
            staged[k, c] = amplitudes_ref[needed_ref[ahead(k), c]]
        amp_copy(k).start()

    def multiply(i):
        @pl.loop(0, slots)
        def _(j):
            rank = rank_ref[p, j]
            chosen = got[i, 0]
            for c in range(1, capacity):
                chosen = jnp.where(rank == c, got[i, c], chosen)
            product[...] = jnp.dot(chosen, slab_data[j], preferred_element_type=jnp.float32)
            for e in range(slab_count):
                start = pl.multiple_of(lax.rem(s + e, slab_count) * share, share)
                rows = product[pl.ds(start, share), :]
                if e == 0:
                    own[i, j] = rows
                else:
                    code, scale = quantize(rows)
                    part_out[i, e - 1, j] = code
                    part_out_scale[i, e - 1, pl.ds(j, 1), :] = scale

        for e in range(1, slab_count):
            for copy in part_copies(i, e):
                copy.start()

    def add_up(i, codes, scales, first):
        for e in range(1, slab_count):
            for copy in part_copies(i, e):
                copy.wait_recv()

        @pl.loop(0, slots)
        def _(j):
            total = own[i, j]
            for e in range(1, slab_count):
                total += widen(part_in[i, e - 1, j], part_in_scale[i, e - 1, pl.ds(j, 1), :])
            code, scale = quantize(total)
            codes[first + j] = code
            scales[pl.ds(first + j, 1), :] = scale

    def return_rows(i):
        add_up(i, back_out.at[i], back_out_scale.at[i], 0)
        for copy in back_copies(i):
            copy.start()

    for k in range(1, min(window, planes - 1) + 1):
        send_amplitudes(k)
    for c in range(capacity):
        got[0, c] = amplitudes_ref[needed_ref[p, c]]
    relay_copy(0).start()
    for j in range(slots):
        load(j).wait()
    multiply(0)
    relay_copy(0).wait_recv()
    multiply(1)
    add_up(0, back_in, back_in_scale, p * slots)

    @pl.loop(1, planes)
    def _(k):
        amp_copy(k).wait_recv()
        relay_copy(k).start()

        @pl.when(k + window < planes)
        def _():
            send_amplitudes(k + window)

        multiply(2 * k)
        return_rows(2 * k - 1)
        relay_copy(k).wait_recv()
        multiply(2 * k + 1)
        return_rows(2 * k)

    return_rows(pair_count - 1)

    @pl.loop(1, pair_count)
    def _(i):
        for copy in back_copies(i):
            copy.wait_recv()

    columns = lax.broadcasted_iota(jnp.int32, (share, width), 1)

    @pl.loop(0, block_count)
    def _(b):
        k = inverse_ref[b]
        ladder = widen(back_in[k], back_in_scale[pl.ds(k, 1), :])
        occ = jnp.concatenate([occ_ref[label_ref[b]]] * (width // tile_width), axis=1)
        divisor = vir_ref[pl.ds(b, 1), :] - occ
        value = (ladder + other_ref[b].astype(jnp.float32)) / divisor
        live = columns < tile_width * tiles_ref[b]
        out_ref[b] = jnp.where(live, value, jnp.zeros_like(value)).astype(out_ref.dtype)

    @pl.loop(1, planes)
    def _(k):
        amp_copy(k).wait_send()

    @pl.loop(0, planes)
    def _(k):
        relay_copy(k).wait_send()

    @pl.loop(1, pair_count)
    def _(i):
        for copy in back_copies(i):
            copy.wait_send()

    @pl.loop(0, pair_count)
    def _(i):
        for e in range(1, slab_count):
            for copy in part_copies(i, e):
                copy.wait_send()


def kernel_path(capacity, amplitudes, integrals, other_terms, occ_energy, vir_energy, block_tiles, block_irrep, inverse, needed, rank):
    n = lax.axis_size("pair")
    m = lax.axis_size("slab")
    slots, depth, width = integrals.shape
    rows = amplitudes.shape[2]
    share = rows // m
    blocks = n * slots
    turned = jnp.swapaxes(amplitudes, 1, 2)
    occ_wide = jnp.broadcast_to(occ_energy[:, :, None], occ_energy.shape + (tile_width,))
    smem = pl.BlockSpec(memory_space=pltpu.SMEM)
    vmem = pl.BlockSpec(memory_space=pltpu.VMEM)
    f32, i16, bf16 = jnp.float32, jnp.int16, jnp.bfloat16
    return pl.pallas_call(
        functools.partial(ladder_kernel, n, m, capacity),
        out_shape=jax.ShapeDtypeStruct(other_terms.shape, bf16),
        in_specs=[smem] * 5 + [vmem, pl.BlockSpec(memory_space=pl.ANY)] + [vmem] * 3,
        out_specs=vmem,
        scratch_shapes=[
            pltpu.VMEM((slots, depth, width), bf16),
            pltpu.VMEM((n // 2, capacity, rows, depth), bf16),
            pltpu.VMEM((n, capacity, rows, depth), bf16),
            pltpu.VMEM((rows, width), f32),
            pltpu.VMEM((n, slots, share, width), f32),
            pltpu.VMEM((n, m - 1, slots, share, width), i16),
            pltpu.VMEM((n, m - 1, slots, width), f32),
            pltpu.VMEM((n, m - 1, slots, share, width), i16),
            pltpu.VMEM((n, m - 1, slots, width), f32),
            pltpu.VMEM((n, slots, share, width), i16),
            pltpu.VMEM((n, slots, width), f32),
            pltpu.VMEM((blocks, share, width), i16),
            pltpu.VMEM((blocks, width), f32),
            pltpu.SemaphoreType.DMA((slots,)),
            pltpu.SemaphoreType.DMA((2, n)),
            pltpu.SemaphoreType.DMA((2, n, m - 1)),
            pltpu.SemaphoreType.DMA((2, n, m - 1)),
            pltpu.SemaphoreType.DMA((2, n)),
            pltpu.SemaphoreType.DMA((2, n)),
        ],
        compiler_params=pltpu.CompilerParams(
            collective_id=capacity, has_side_effects=True, vmem_limit_bytes=50 * 1024 * 1024
        ),
        cost_estimate=pl.CostEstimate(
            flops=2 * slots * n * rows * depth * width, bytes_accessed=2 * slots * depth * width, transcendentals=0
        ),
    )(needed, rank, inverse, block_irrep, block_tiles, turned, integrals, other_terms, occ_wide, vir_energy)


def shards(
    amplitudes,
    integrals,
    other_terms,
    occ_energy,
    vir_energy,
    block_tiles,
    block_irrep,
    block_order,
):
    whole = (amplitudes, integrals, other_terms, occ_energy, vir_energy, block_tiles, block_irrep, block_order)
    n = lax.axis_size("pair")
    slots = integrals.shape[0]
    share = amplitudes.shape[2] // lax.axis_size("slab")
    if share % 16 or slots % 8 or n % 4 or n > 16:
        return gathered_path(*whole)
    numbers = jnp.arange(n * slots, dtype=jnp.int32)
    inverse = jnp.sum(jnp.where(block_order[None, :] == numbers[:, None], numbers[None, :], 0), axis=1)
    labels = jnp.sum(jnp.where(block_order[:, None] == numbers[None, :], block_irrep[None, :], 0), axis=1)
    labels = labels.reshape(n // 2, 2 * slots)
    changed = (labels[:, 1:] != labels[:, :-1]).astype(jnp.int32)
    order = jnp.arange(2 * slots, dtype=jnp.int32)
    changed = jnp.pad(changed, ((0, 0), (1, 0)))
    rank = jnp.sum(jnp.where(order[None, None, :] <= order[None, :, None], changed[:, None, :], 0), axis=2)
    most = jnp.max(rank) + 1

    def run(capacity):
        places = jnp.arange(capacity, dtype=jnp.int32)
        needed = jnp.max(jnp.where(rank[:, :, None] == places, labels[:, :, None], 0), axis=1)
        needed = jnp.repeat(needed, 2, axis=0)
        return lambda: kernel_path(
            capacity, amplitudes, integrals, other_terms, occ_energy, vir_energy, block_tiles, block_irrep, inverse, needed, rank.reshape(n, slots)
        )

    choice = jnp.clip(most - 3, 0, 3)
    return lax.switch(choice, [run(3), run(4), run(5), lambda: gathered_path(*whole)])


def solution(mesh):
    return jax.shard_map(
        shards,
        mesh=mesh,
        in_specs=(
            P(None, "slab", "pair"),
            P("pair", "slab", None),
            P(None, ("pair", "slab"), None),
            P(None, ("pair", "slab")),
            P(),
            P(),
            P(),
            P(),
        ),
        out_specs=P(None, ("pair", "slab"), None),
        check_vma=False,
    )
```

```python
import functools

import jax
import jax.numpy as jnp
from jax import lax
from jax.sharding import PartitionSpec as P

from jax.experimental import pallas as pl
from jax.experimental.pallas import tpu as pltpu

tile_width = 128
quant_top = 32766.0
quant_floor = 1e-33
window = 3
relay_window = 2


def gathered_path(
    amplitudes,
    integrals,
    other_terms,
    occ_energy,
    vir_energy,
    block_tiles,
    block_irrep,
    block_order,
):
    pair_count = lax.axis_size("pair")
    slab_count = lax.axis_size("slab")
    slot_count, cd_local, width_max = integrals.shape
    first_slot = lax.axis_index("pair") * slot_count
    my_blocks = lax.dynamic_slice_in_dim(block_order, first_slot, slot_count)
    my_labels = jnp.take(block_irrep, my_blocks)
    chosen = jnp.take(lax.all_gather(amplitudes, "pair", axis=2, tiled=True), my_labels, axis=0)
    ladder = jnp.einsum("bkr,bkw->brw", chosen, integrals, preferred_element_type=jnp.float32)
    row_share = ladder.shape[1] // (pair_count * slab_count)
    ladder = ladder.reshape(slot_count, pair_count, slab_count, row_share, width_max)
    total = lax.psum(ladder, "slab")
    my_share = lax.dynamic_slice_in_dim(total, lax.axis_index("slab"), 1, 2)
    returned = lax.all_to_all(my_share, "pair", split_axis=1, concat_axis=0, tiled=True)
    returned = returned.reshape(pair_count * slot_count, row_share, width_max)
    inverse = jnp.argsort(block_order)
    ordered = jnp.take(returned, inverse, axis=0)
    label_count = occ_energy.shape[0]
    one_hot = (block_irrep[:, None] == jnp.arange(label_count, dtype=jnp.int32)[None, :]).astype(
        jnp.float32
    )
    occ_rows = jnp.dot(one_hot, occ_energy, precision=lax.Precision.HIGHEST)
    divisor = vir_energy[:, None, :] - occ_rows[:, :, None]
    columns = jnp.arange(width_max, dtype=jnp.int32)
    live_mask = columns[None, None, :] < (tile_width * block_tiles)[:, None, None]
    value = (ordered + other_terms.astype(jnp.float32)) / divisor
    return jnp.where(live_mask, value, jnp.zeros_like(value)).astype(jnp.bfloat16)


def quantize(value):
    top = jnp.maximum(jnp.max(jnp.abs(value), axis=0, keepdims=True), quant_floor)
    code = jnp.round(value * (quant_top / top)).astype(jnp.int32).astype(jnp.int16)
    return code, top * (1.0 / quant_top)


def widen(code, scale):
    return code.astype(jnp.int32).astype(jnp.float32) * scale


def ladder_kernel(
    pair_count,
    slab_count,
    capacity,
    needed_ref,
    rank_ref,
    inverse_ref,
    label_ref,
    tiles_ref,
    amplitudes_ref,
    integrals_ref,
    other_ref,
    occ_ref,
    vir_ref,
    out_ref,
    slab_data,
    staged,
    got,
    product,
    own,
    part_out,
    part_out_scale,
    part_in,
    part_in_scale,
    back_out,
    back_out_scale,
    back_in,
    back_in_scale,
    slab_sem,
    amp_sems,
    part_sems,
    part_scale_sems,
    back_sems,
    back_scale_sems,
):
    slots = integrals_ref.shape[0]
    share = own.shape[2]
    width = own.shape[3]
    block_count = out_ref.shape[0]
    p = lax.axis_index("pair")
    s = lax.axis_index("slab")

    def load(j):
        return pltpu.make_async_copy(integrals_ref.at[j], slab_data.at[j], slab_sem.at[j])

    for j in range(slots):
        load(j).start()

    barrier = pltpu.get_barrier_semaphore()
    for d in range(1, pair_count):
        pl.semaphore_signal(barrier, inc=1, device_id=(lax.rem(p + d, pair_count), s), device_id_type=pl.DeviceIdType.MESH)
    for e in range(1, slab_count):
        pl.semaphore_signal(barrier, inc=1, device_id=(p, lax.rem(s + e, slab_count)), device_id_type=pl.DeviceIdType.MESH)
    pl.semaphore_wait(barrier, pair_count + slab_count - 2)

    def distance(i):
        return i // 2 + lax.rem(i, 2) * (pair_count // 2)

    def ahead(i):
        return lax.rem(p + distance(i), pair_count)

    def behind(i):
        return lax.rem(p + pair_count - distance(i), pair_count)

    def remote(source, target, sems, at, device):
        return pltpu.make_async_remote_copy(
            src_ref=source,
            dst_ref=target,
            send_sem=sems.at[(0,) + at],
            recv_sem=sems.at[(1,) + at],
            device_id=device,
            device_id_type=pl.DeviceIdType.MESH,
        )

    def amp_copy(i):
        return remote(staged.at[i], got.at[i], amp_sems, (i,), (ahead(i), s))

    def part_copies(i, e):
        device = (p, lax.rem(s + e, slab_count))
        return (
            remote(part_out.at[i, e - 1], part_in.at[i, e - 1], part_sems, (i, e - 1), device),
            remote(part_out_scale.at[i, e - 1], part_in_scale.at[i, e - 1], part_scale_sems, (i, e - 1), device),
        )

    mine = pl.ds(pl.multiple_of(p * slots, slots), slots)

    def back_copies(i):
        device = (behind(i), s)
        return (
            remote(back_out.at[i], back_in.at[mine], back_sems, (i,), device),
            remote(back_out_scale.at[i], back_in_scale.at[mine], back_scale_sems, (i,), device),
        )

    def send_amplitudes(i):
        for c in range(capacity):
            staged[i, c] = amplitudes_ref[needed_ref[ahead(i), c]]
        amp_copy(i).start()

    def multiply(i):
        @pl.loop(0, slots)
        def _(j):
            rank = rank_ref[p, j]
            chosen = got[i, 0]
            for c in range(1, capacity):
                chosen = jnp.where(rank == c, got[i, c], chosen)
            product[...] = jnp.dot(chosen, slab_data[j], preferred_element_type=jnp.float32)
            for e in range(slab_count):
                start = pl.multiple_of(lax.rem(s + e, slab_count) * share, share)
                rows = product[pl.ds(start, share), :]
                if e == 0:
                    own[i, j] = rows
                else:
                    code, scale = quantize(rows)
                    part_out[i, e - 1, j] = code
                    part_out_scale[i, e - 1, pl.ds(j, 1), :] = scale

        for e in range(1, slab_count):
            for copy in part_copies(i, e):
                copy.start()

    def add_up(i, codes, scales, first):
        for e in range(1, slab_count):
            for copy in part_copies(i, e):
                copy.wait_recv()

        @pl.loop(0, slots)
        def _(j):
            total = own[i, j]
            for e in range(1, slab_count):
                total += widen(part_in[i, e - 1, j], part_in_scale[i, e - 1, pl.ds(j, 1), :])
            code, scale = quantize(total)
            codes[first + j] = code
            scales[pl.ds(first + j, 1), :] = scale

    def return_rows(i):
        add_up(i, back_out.at[i], back_out_scale.at[i], 0)
        for copy in back_copies(i):
            copy.start()

    for i in range(1, min(window, pair_count - 1) + 1):
        send_amplitudes(i)
    for c in range(capacity):
        got[0, c] = amplitudes_ref[needed_ref[p, c]]
    for j in range(slots):
        load(j).wait()
    multiply(0)

    @pl.loop(1, pair_count)
    def _(i):
        amp_copy(i).wait_recv()

        @pl.when(i + window < pair_count)
        def _():
            send_amplitudes(i + window)

        multiply(i)

        @pl.when(i == 1)
        def _():
            add_up(0, back_in, back_in_scale, p * slots)

        @pl.when(i > 1)
        def _():
            return_rows(i - 1)

    return_rows(pair_count - 1)

    @pl.loop(1, pair_count)
    def _(i):
        for copy in back_copies(i):
            copy.wait_recv()

    columns = lax.broadcasted_iota(jnp.int32, (share, width), 1)

    @pl.loop(0, block_count)
    def _(b):
        k = inverse_ref[b]
        ladder = widen(back_in[k], back_in_scale[pl.ds(k, 1), :])
        occ = jnp.concatenate([occ_ref[label_ref[b]]] * (width // tile_width), axis=1)
        divisor = vir_ref[pl.ds(b, 1), :] - occ
        value = (ladder + other_ref[b].astype(jnp.float32)) / divisor
        live = columns < tile_width * tiles_ref[b]
        out_ref[b] = jnp.where(live, value, jnp.zeros_like(value)).astype(out_ref.dtype)

    @pl.loop(1, pair_count)
    def _(i):
        amp_copy(i).wait_send()
        for copy in back_copies(i):
            copy.wait_send()

    @pl.loop(0, pair_count)
    def _(i):
        for e in range(1, slab_count):
            for copy in part_copies(i, e):
                copy.wait_send()


def relay_kernel(
    pair_count,
    slab_count,
    capacity,
    needed_ref,
    rank_ref,
    inverse_ref,
    label_ref,
    tiles_ref,
    amplitudes_ref,
    integrals_ref,
    other_ref,
    occ_ref,
    vir_ref,
    out_ref,
    slab_data,
    staged,
    got,
    product,
    own,
    part_out,
    part_out_scale,
    part_in,
    part_in_scale,
    back_out,
    back_out_scale,
    back_in,
    back_in_scale,
    slab_sem,
    amp_sems,
    part_sems,
    part_scale_sems,
    back_sems,
    back_scale_sems,
):
    slots = integrals_ref.shape[0]
    share = own.shape[2]
    width = own.shape[3]
    block_count = out_ref.shape[0]
    p = lax.axis_index("pair")
    s = lax.axis_index("slab")

    def load(j):
        return pltpu.make_async_copy(integrals_ref.at[j], slab_data.at[j], slab_sem.at[j])

    for j in range(slots):
        load(j).start()

    barrier = pltpu.get_barrier_semaphore()
    for d in range(1, pair_count):
        pl.semaphore_signal(barrier, inc=1, device_id=(lax.rem(p + d, pair_count), s), device_id_type=pl.DeviceIdType.MESH)
    for e in range(1, slab_count):
        pl.semaphore_signal(barrier, inc=1, device_id=(p, lax.rem(s + e, slab_count)), device_id_type=pl.DeviceIdType.MESH)
    pl.semaphore_wait(barrier, pair_count + slab_count - 2)

    planes = pair_count // 2
    plane, side = p // 2, lax.rem(p, 2)
    partner = 2 * plane + 1 - side

    def distance(k):
        return k // 2 + lax.rem(k, 2) * (planes // 2)

    def ahead(k):
        return 2 * lax.rem(plane + distance(k), planes) + side

    def behind(i):
        return 2 * lax.rem(plane + planes - distance(i // 2), planes) + lax.rem(side + lax.rem(i, 2), 2)

    def remote(source, target, sems, at, device):
        return pltpu.make_async_remote_copy(
            src_ref=source,
            dst_ref=target,
            send_sem=sems.at[(0,) + at],
            recv_sem=sems.at[(1,) + at],
            device_id=device,
            device_id_type=pl.DeviceIdType.MESH,
        )

    def amp_copy(k):
        return remote(staged.at[k], got.at[2 * k], amp_sems, (2 * k,), (ahead(k), s))

    def relay_copy(k):
        return remote(got.at[2 * k], got.at[2 * k + 1], amp_sems, (2 * k + 1,), (partner, s))

    def part_copies(i, e):
        device = (p, lax.rem(s + e, slab_count))
        return (
            remote(part_out.at[i, e - 1], part_in.at[i, e - 1], part_sems, (i, e - 1), device),
            remote(part_out_scale.at[i, e - 1], part_in_scale.at[i, e - 1], part_scale_sems, (i, e - 1), device),
        )

    mine = pl.ds(pl.multiple_of(p * slots, slots), slots)

    def back_copies(i):
        device = (behind(i), s)
        return (
            remote(back_out.at[i], back_in.at[mine], back_sems, (i,), device),
            remote(back_out_scale.at[i], back_in_scale.at[mine], back_scale_sems, (i,), device),
        )

    def send_amplitudes(k):
        for c in range(capacity):
            staged[k, c] = amplitudes_ref[needed_ref[ahead(k), c]]
        amp_copy(k).start()

    def multiply(i):
        @pl.loop(0, slots)
        def _(j):
            rank = rank_ref[p, j]
            chosen = got[i, 0]
            for c in range(1, capacity):
                chosen = jnp.where(rank == c, got[i, c], chosen)
            product[...] = jnp.dot(chosen, slab_data[j], preferred_element_type=jnp.float32)
            for e in range(slab_count):
                start = pl.multiple_of(lax.rem(s + e, slab_count) * share, share)
                rows = product[pl.ds(start, share), :]
                if e == 0:
                    own[i, j] = rows
                else:
                    code, scale = quantize(rows)
                    part_out[i, e - 1, j] = code
                    part_out_scale[i, e - 1, pl.ds(j, 1), :] = scale

        for e in range(1, slab_count):
            for copy in part_copies(i, e):
                copy.start()

    def add_up(i, codes, scales, first):
        for e in range(1, slab_count):
            for copy in part_copies(i, e):
                copy.wait_recv()

        @pl.loop(0, slots)
        def _(j):
            total = own[i, j]
            for e in range(1, slab_count):
                total += widen(part_in[i, e - 1, j], part_in_scale[i, e - 1, pl.ds(j, 1), :])
            code, scale = quantize(total)
            codes[first + j] = code
            scales[pl.ds(first + j, 1), :] = scale

    def return_rows(i):
        add_up(i, back_out.at[i], back_out_scale.at[i], 0)
        for copy in back_copies(i):
            copy.start()

    for k in range(1, min(relay_window, planes - 1) + 1):
        send_amplitudes(k)
    for c in range(capacity):
        got[0, c] = amplitudes_ref[needed_ref[p, c]]
    relay_copy(0).start()
    for j in range(slots):
        load(j).wait()
    multiply(0)
    relay_copy(0).wait_recv()
    multiply(1)
    add_up(0, back_in, back_in_scale, p * slots)

    @pl.loop(1, planes)
    def _(k):
        amp_copy(k).wait_recv()
        relay_copy(k).start()

        @pl.when(k + relay_window < planes)
        def _():
            send_amplitudes(k + relay_window)

        multiply(2 * k)
        return_rows(2 * k - 1)
        relay_copy(k).wait_recv()
        multiply(2 * k + 1)
        return_rows(2 * k)

    return_rows(pair_count - 1)

    @pl.loop(1, pair_count)
    def _(i):
        for copy in back_copies(i):
            copy.wait_recv()

    columns = lax.broadcasted_iota(jnp.int32, (share, width), 1)

    @pl.loop(0, block_count)
    def _(b):
        k = inverse_ref[b]
        ladder = widen(back_in[k], back_in_scale[pl.ds(k, 1), :])
        occ = jnp.concatenate([occ_ref[label_ref[b]]] * (width // tile_width), axis=1)
        divisor = vir_ref[pl.ds(b, 1), :] - occ
        value = (ladder + other_ref[b].astype(jnp.float32)) / divisor
        live = columns < tile_width * tiles_ref[b]
        out_ref[b] = jnp.where(live, value, jnp.zeros_like(value)).astype(out_ref.dtype)

    @pl.loop(1, planes)
    def _(k):
        amp_copy(k).wait_send()

    @pl.loop(0, planes)
    def _(k):
        relay_copy(k).wait_send()

    @pl.loop(1, pair_count)
    def _(i):
        for copy in back_copies(i):
            copy.wait_send()

    @pl.loop(0, pair_count)
    def _(i):
        for e in range(1, slab_count):
            for copy in part_copies(i, e):
                copy.wait_send()


def kernel_path(kernel, capacity, amplitudes, integrals, other_terms, occ_energy, vir_energy, block_tiles, block_irrep, inverse, needed, rank):
    n = lax.axis_size("pair")
    m = lax.axis_size("slab")
    slots, depth, width = integrals.shape
    rows = amplitudes.shape[2]
    share = rows // m
    blocks = n * slots
    turned = jnp.swapaxes(amplitudes, 1, 2)
    occ_wide = jnp.broadcast_to(occ_energy[:, :, None], occ_energy.shape + (tile_width,))
    smem = pl.BlockSpec(memory_space=pltpu.SMEM)
    vmem = pl.BlockSpec(memory_space=pltpu.VMEM)
    f32, i16, bf16 = jnp.float32, jnp.int16, jnp.bfloat16
    return pl.pallas_call(
        functools.partial(kernel, n, m, capacity),
        out_shape=jax.ShapeDtypeStruct(other_terms.shape, bf16),
        in_specs=[smem] * 5 + [vmem, pl.BlockSpec(memory_space=pl.ANY)] + [vmem] * 3,
        out_specs=vmem,
        scratch_shapes=[
            pltpu.VMEM((slots, depth, width), bf16),
            pltpu.VMEM((n, capacity, rows, depth), bf16),
            pltpu.VMEM((n, capacity, rows, depth), bf16),
            pltpu.VMEM((rows, width), f32),
            pltpu.VMEM((n, slots, share, width), f32),
            pltpu.VMEM((n, m - 1, slots, share, width), i16),
            pltpu.VMEM((n, m - 1, slots, width), f32),
            pltpu.VMEM((n, m - 1, slots, share, width), i16),
            pltpu.VMEM((n, m - 1, slots, width), f32),
            pltpu.VMEM((n, slots, share, width), i16),
            pltpu.VMEM((n, slots, width), f32),
            pltpu.VMEM((blocks, share, width), i16),
            pltpu.VMEM((blocks, width), f32),
            pltpu.SemaphoreType.DMA((slots,)),
            pltpu.SemaphoreType.DMA((2, n)),
            pltpu.SemaphoreType.DMA((2, n, m - 1)),
            pltpu.SemaphoreType.DMA((2, n, m - 1)),
            pltpu.SemaphoreType.DMA((2, n)),
            pltpu.SemaphoreType.DMA((2, n)),
        ],
        compiler_params=pltpu.CompilerParams(
            collective_id=capacity, has_side_effects=True, vmem_limit_bytes=50 * 1024 * 1024
        ),
        cost_estimate=pl.CostEstimate(
            flops=2 * slots * n * rows * depth * width, bytes_accessed=2 * slots * depth * width, transcendentals=0
        ),
    )(needed, rank, inverse, block_irrep, block_tiles, turned, integrals, other_terms, occ_wide, vir_energy)


def shards(
    amplitudes,
    integrals,
    other_terms,
    occ_energy,
    vir_energy,
    block_tiles,
    block_irrep,
    block_order,
):
    whole = (amplitudes, integrals, other_terms, occ_energy, vir_energy, block_tiles, block_irrep, block_order)
    n = lax.axis_size("pair")
    slots = integrals.shape[0]
    share = amplitudes.shape[2] // lax.axis_size("slab")
    if share % 16 or slots % 8 or n % 4 or n > 16:
        return gathered_path(*whole)
    numbers = jnp.arange(n * slots, dtype=jnp.int32)
    inverse = jnp.sum(jnp.where(block_order[None, :] == numbers[:, None], numbers[None, :], 0), axis=1)
    labels = jnp.sum(jnp.where(block_order[:, None] == numbers[None, :], block_irrep[None, :], 0), axis=1)

    def ranks(group):
        held = labels.reshape(-1, group)
        changed = (held[:, 1:] != held[:, :-1]).astype(jnp.int32)
        changed = jnp.pad(changed, ((0, 0), (1, 0)))
        order = jnp.arange(group, dtype=jnp.int32)
        upto = order[None, None, :] <= order[None, :, None]
        return jnp.sum(jnp.where(upto, changed[:, None, :], 0), axis=2)

    device_rank, plane_rank = ranks(slots), ranks(2 * slots)

    def run(kernel, capacity, rank):
        group = rank.shape[1]
        places = jnp.arange(capacity, dtype=jnp.int32)
        held = labels.reshape(-1, group)
        needed = jnp.max(jnp.where(rank[:, :, None] == places, held[:, :, None], 0), axis=1)
        needed = jnp.repeat(needed, group // slots, axis=0)
        places_of = rank.reshape(n, slots)
        return lambda: kernel_path(
            kernel, capacity, amplitudes, integrals, other_terms, occ_energy, vir_energy, block_tiles, block_irrep, inverse, needed, places_of
        )

    relayed = jnp.clip(jnp.max(plane_rank) - 1, 1, 4)
    choice = jnp.where(jnp.max(device_rank) < 2, 0, relayed)
    return lax.switch(
        choice,
        [
            run(ladder_kernel, 2, device_rank),
            run(relay_kernel, 3, plane_rank),
            run(relay_kernel, 4, plane_rank),
            run(relay_kernel, 5, plane_rank),
            lambda: gathered_path(*whole),
        ],
    )


def solution(mesh):
    return jax.shard_map(
        shards,
        mesh=mesh,
        in_specs=(
            P(None, "slab", "pair"),
            P("pair", "slab", None),
            P(None, ("pair", "slab"), None),
            P(None, ("pair", "slab")),
            P(),
            P(),
            P(),
            P(),
        ),
        out_specs=P(None, ("pair", "slab"), None),
        check_vma=False,
    )
```

```python
import functools

import jax
import jax.numpy as jnp
from jax import lax
from jax.sharding import PartitionSpec as P

from jax.experimental import pallas as pl
from jax.experimental.pallas import tpu as pltpu

tile_width = 128
quant_top = 32766.0
quant_floor = 1e-33
window = 7
relay_window = 2


def gathered_path(
    amplitudes,
    integrals,
    other_terms,
    occ_energy,
    vir_energy,
    block_tiles,
    block_irrep,
    block_order,
):
    pair_count = lax.axis_size("pair")
    slab_count = lax.axis_size("slab")
    slot_count, cd_local, width_max = integrals.shape
    first_slot = lax.axis_index("pair") * slot_count
    my_blocks = lax.dynamic_slice_in_dim(block_order, first_slot, slot_count)
    my_labels = jnp.take(block_irrep, my_blocks)
    chosen = jnp.take(lax.all_gather(amplitudes, "pair", axis=2, tiled=True), my_labels, axis=0)
    ladder = jnp.einsum("bkr,bkw->brw", chosen, integrals, preferred_element_type=jnp.float32)
    row_share = ladder.shape[1] // (pair_count * slab_count)
    ladder = ladder.reshape(slot_count, pair_count, slab_count, row_share, width_max)
    total = lax.psum(ladder, "slab")
    my_share = lax.dynamic_slice_in_dim(total, lax.axis_index("slab"), 1, 2)
    returned = lax.all_to_all(my_share, "pair", split_axis=1, concat_axis=0, tiled=True)
    returned = returned.reshape(pair_count * slot_count, row_share, width_max)
    inverse = jnp.argsort(block_order)
    ordered = jnp.take(returned, inverse, axis=0)
    label_count = occ_energy.shape[0]
    one_hot = (block_irrep[:, None] == jnp.arange(label_count, dtype=jnp.int32)[None, :]).astype(
        jnp.float32
    )
    occ_rows = jnp.dot(one_hot, occ_energy, precision=lax.Precision.HIGHEST)
    divisor = vir_energy[:, None, :] - occ_rows[:, :, None]
    columns = jnp.arange(width_max, dtype=jnp.int32)
    live_mask = columns[None, None, :] < (tile_width * block_tiles)[:, None, None]
    value = (ordered + other_terms.astype(jnp.float32)) / divisor
    return jnp.where(live_mask, value, jnp.zeros_like(value)).astype(jnp.bfloat16)


def quantize(value):
    top = jnp.maximum(jnp.max(jnp.abs(value), axis=0, keepdims=True), quant_floor)
    code = jnp.round(value * (quant_top / top)).astype(jnp.int32).astype(jnp.int16)
    return code, top * (1.0 / quant_top)


def widen(code, scale):
    return code.astype(jnp.int32).astype(jnp.float32) * scale


def ladder_kernel(
    pair_count,
    slab_count,
    capacity,
    needed_ref,
    rank_ref,
    inverse_ref,
    label_ref,
    tiles_ref,
    amplitudes_ref,
    integrals_ref,
    other_ref,
    occ_ref,
    vir_ref,
    out_ref,
    slab_data,
    staged,
    got,
    product,
    own,
    part_out,
    part_out_scale,
    part_in,
    part_in_scale,
    back_out,
    back_out_scale,
    back_in,
    back_in_scale,
    slab_sem,
    amp_sems,
    part_sems,
    part_scale_sems,
    back_sems,
    back_scale_sems,
):
    slots = integrals_ref.shape[0]
    share = own.shape[2]
    width = own.shape[3]
    block_count = out_ref.shape[0]
    p = lax.axis_index("pair")
    s = lax.axis_index("slab")

    def load(j):
        return pltpu.make_async_copy(integrals_ref.at[j], slab_data.at[j], slab_sem.at[j])

    for j in range(slots):
        load(j).start()

    barrier = pltpu.get_barrier_semaphore()
    for d in range(1, pair_count):
        pl.semaphore_signal(barrier, inc=1, device_id=(lax.rem(p + d, pair_count), s), device_id_type=pl.DeviceIdType.MESH)
    for e in range(1, slab_count):
        pl.semaphore_signal(barrier, inc=1, device_id=(p, lax.rem(s + e, slab_count)), device_id_type=pl.DeviceIdType.MESH)
    pl.semaphore_wait(barrier, pair_count + slab_count - 2)

    def distance(i):
        return i // 2 + lax.rem(i, 2) * (pair_count // 2)

    def ahead(i):
        return lax.rem(p + distance(i), pair_count)

    def behind(i):
        return lax.rem(p + pair_count - distance(i), pair_count)

    def remote(source, target, sems, at, device):
        return pltpu.make_async_remote_copy(
            src_ref=source,
            dst_ref=target,
            send_sem=sems.at[(0,) + at],
            recv_sem=sems.at[(1,) + at],
            device_id=device,
            device_id_type=pl.DeviceIdType.MESH,
        )

    def amp_copy(i):
        return remote(staged.at[i], got.at[i], amp_sems, (i,), (ahead(i), s))

    def part_copies(i, e):
        device = (p, lax.rem(s + e, slab_count))
        return (
            remote(part_out.at[i, e - 1], part_in.at[i, e - 1], part_sems, (i, e - 1), device),
            remote(part_out_scale.at[i, e - 1], part_in_scale.at[i, e - 1], part_scale_sems, (i, e - 1), device),
        )

    mine = pl.ds(pl.multiple_of(p * slots, slots), slots)

    def back_copies(i):
        device = (behind(i), s)
        return (
            remote(back_out.at[i], back_in.at[mine], back_sems, (i,), device),
            remote(back_out_scale.at[i], back_in_scale.at[mine], back_scale_sems, (i,), device),
        )

    def send_amplitudes(i):
        for c in range(capacity):
            staged[i, c] = amplitudes_ref[needed_ref[ahead(i), c]]
        amp_copy(i).start()

    def multiply(i):
        @pl.loop(0, slots)
        def _(j):
            rank = rank_ref[p, j]
            chosen = got[i, 0]
            for c in range(1, capacity):
                chosen = jnp.where(rank == c, got[i, c], chosen)
            product[...] = jnp.dot(chosen, slab_data[j], preferred_element_type=jnp.float32)
            for e in range(slab_count):
                start = pl.multiple_of(lax.rem(s + e, slab_count) * share, share)
                rows = product[pl.ds(start, share), :]
                if e == 0:
                    own[i, j] = rows
                else:
                    code, scale = quantize(rows)
                    part_out[i, e - 1, j] = code
                    part_out_scale[i, e - 1, pl.ds(j, 1), :] = scale

        for e in range(1, slab_count):
            for copy in part_copies(i, e):
                copy.start()

    def add_up(i, codes, scales, first):
        for e in range(1, slab_count):
            for copy in part_copies(i, e):
                copy.wait_recv()

        @pl.loop(0, slots)
        def _(j):
            total = own[i, j]
            for e in range(1, slab_count):
                total += widen(part_in[i, e - 1, j], part_in_scale[i, e - 1, pl.ds(j, 1), :])
            code, scale = quantize(total)
            codes[first + j] = code
            scales[pl.ds(first + j, 1), :] = scale

    def return_rows(i):
        add_up(i, back_out.at[i], back_out_scale.at[i], 0)
        for copy in back_copies(i):
            copy.start()

    for i in range(1, min(window, pair_count - 1) + 1):
        send_amplitudes(i)
    for c in range(capacity):
        got[0, c] = amplitudes_ref[needed_ref[p, c]]
    for j in range(slots):
        load(j).wait()
    multiply(0)

    @pl.loop(1, pair_count)
    def _(i):
        amp_copy(i).wait_recv()

        @pl.when(i + window < pair_count)
        def _():
            send_amplitudes(i + window)

        multiply(i)

        @pl.when(i == 1)
        def _():
            add_up(0, back_in, back_in_scale, p * slots)

        @pl.when(i > 1)
        def _():
            return_rows(i - 1)

    return_rows(pair_count - 1)

    @pl.loop(1, pair_count)
    def _(i):
        for copy in back_copies(i):
            copy.wait_recv()

    columns = lax.broadcasted_iota(jnp.int32, (share, width), 1)

    @pl.loop(0, block_count, unroll=4)
    def _(b):
        k = inverse_ref[b]
        ladder = widen(back_in[k], back_in_scale[pl.ds(k, 1), :])
        occ = jnp.concatenate([occ_ref[label_ref[b]]] * (width // tile_width), axis=1)
        divisor = vir_ref[pl.ds(b, 1), :] - occ
        value = (ladder + other_ref[b].astype(jnp.float32)) / divisor
        live = columns < tile_width * tiles_ref[b]
        out_ref[b] = jnp.where(live, value, jnp.zeros_like(value)).astype(out_ref.dtype)

    @pl.loop(1, pair_count)
    def _(i):
        amp_copy(i).wait_send()
        for copy in back_copies(i):
            copy.wait_send()

    @pl.loop(0, pair_count)
    def _(i):
        for e in range(1, slab_count):
            for copy in part_copies(i, e):
                copy.wait_send()


def relay_kernel(
    pair_count,
    slab_count,
    capacity,
    needed_ref,
    rank_ref,
    inverse_ref,
    label_ref,
    tiles_ref,
    amplitudes_ref,
    integrals_ref,
    other_ref,
    occ_ref,
    vir_ref,
    out_ref,
    slab_data,
    staged,
    got,
    product,
    own,
    part_out,
    part_out_scale,
    part_in,
    part_in_scale,
    back_out,
    back_out_scale,
    back_in,
    back_in_scale,
    slab_sem,
    amp_sems,
    part_sems,
    part_scale_sems,
    back_sems,
    back_scale_sems,
):
    slots = integrals_ref.shape[0]
    share = own.shape[2]
    width = own.shape[3]
    block_count = out_ref.shape[0]
    p = lax.axis_index("pair")
    s = lax.axis_index("slab")

    def load(j):
        return pltpu.make_async_copy(integrals_ref.at[j], slab_data.at[j], slab_sem.at[j])

    for j in range(slots):
        load(j).start()

    barrier = pltpu.get_barrier_semaphore()
    for d in range(1, pair_count):
        pl.semaphore_signal(barrier, inc=1, device_id=(lax.rem(p + d, pair_count), s), device_id_type=pl.DeviceIdType.MESH)
    for e in range(1, slab_count):
        pl.semaphore_signal(barrier, inc=1, device_id=(p, lax.rem(s + e, slab_count)), device_id_type=pl.DeviceIdType.MESH)
    pl.semaphore_wait(barrier, pair_count + slab_count - 2)

    planes = pair_count // 2
    plane, side = p // 2, lax.rem(p, 2)
    partner = 2 * plane + 1 - side

    def distance(k):
        return k

    def ahead(k):
        return 2 * lax.rem(plane + distance(k), planes) + side

    def behind(i):
        return 2 * lax.rem(plane + planes - distance(i // 2), planes) + lax.rem(side + lax.rem(i, 2), 2)

    def remote(source, target, sems, at, device):
        return pltpu.make_async_remote_copy(
            src_ref=source,
            dst_ref=target,
            send_sem=sems.at[(0,) + at],
            recv_sem=sems.at[(1,) + at],
            device_id=device,
            device_id_type=pl.DeviceIdType.MESH,
        )

    def amp_copy(k):
        return remote(staged.at[k], got.at[2 * k], amp_sems, (2 * k,), (ahead(k), s))

    def relay_copy(k):
        return remote(got.at[2 * k], got.at[2 * k + 1], amp_sems, (2 * k + 1,), (partner, s))

    def part_copies(i, e):
        device = (p, lax.rem(s + e, slab_count))
        return (
            remote(part_out.at[i, e - 1], part_in.at[i, e - 1], part_sems, (i, e - 1), device),
            remote(part_out_scale.at[i, e - 1], part_in_scale.at[i, e - 1], part_scale_sems, (i, e - 1), device),
        )

    mine = pl.ds(pl.multiple_of(p * slots, slots), slots)

    def back_copies(i):
        device = (behind(i), s)
        return (
            remote(back_out.at[i], back_in.at[mine], back_sems, (i,), device),
            remote(back_out_scale.at[i], back_in_scale.at[mine], back_scale_sems, (i,), device),
        )

    def send_amplitudes(k):
        for c in range(capacity):
            staged[k, c] = amplitudes_ref[needed_ref[ahead(k), c]]
        amp_copy(k).start()

    def multiply(i):
        @pl.loop(0, slots)
        def _(j):
            rank = rank_ref[p, j]
            chosen = got[i, 0]
            for c in range(1, capacity):
                chosen = jnp.where(rank == c, got[i, c], chosen)
            product[...] = jnp.dot(chosen, slab_data[j], preferred_element_type=jnp.float32)
            for e in range(slab_count):
                start = pl.multiple_of(lax.rem(s + e, slab_count) * share, share)
                rows = product[pl.ds(start, share), :]
                if e == 0:
                    own[i, j] = rows
                else:
                    code, scale = quantize(rows)
                    part_out[i, e - 1, j] = code
                    part_out_scale[i, e - 1, pl.ds(j, 1), :] = scale

        for e in range(1, slab_count):
            for copy in part_copies(i, e):
                copy.start()

    def add_up(i, codes, scales, first):
        for e in range(1, slab_count):
            for copy in part_copies(i, e):
                copy.wait_recv()

        @pl.loop(0, slots)
        def _(j):
            total = own[i, j]
            for e in range(1, slab_count):
                total += widen(part_in[i, e - 1, j], part_in_scale[i, e - 1, pl.ds(j, 1), :])
            code, scale = quantize(total)
            codes[first + j] = code
            scales[pl.ds(first + j, 1), :] = scale

    def return_rows(i):
        add_up(i, back_out.at[i], back_out_scale.at[i], 0)
        for copy in back_copies(i):
            copy.start()

    for k in range(1, min(relay_window, planes - 1) + 1):
        send_amplitudes(k)
    for c in range(capacity):
        got[0, c] = amplitudes_ref[needed_ref[p, c]]
    relay_copy(0).start()
    for j in range(slots):
        load(j).wait()
    multiply(0)
    relay_copy(0).wait_recv()
    multiply(1)
    add_up(0, back_in, back_in_scale, p * slots)

    @pl.loop(1, planes)
    def _(k):
        amp_copy(k).wait_recv()
        relay_copy(k).start()

        @pl.when(k + relay_window < planes)
        def _():
            send_amplitudes(k + relay_window)

        multiply(2 * k)
        return_rows(2 * k - 1)
        relay_copy(k).wait_recv()
        multiply(2 * k + 1)
        return_rows(2 * k)

    return_rows(pair_count - 1)

    @pl.loop(1, pair_count)
    def _(i):
        for copy in back_copies(i):
            copy.wait_recv()

    columns = lax.broadcasted_iota(jnp.int32, (share, width), 1)

    @pl.loop(0, block_count, unroll=4)
    def _(b):
        k = inverse_ref[b]
        ladder = widen(back_in[k], back_in_scale[pl.ds(k, 1), :])
        occ = jnp.concatenate([occ_ref[label_ref[b]]] * (width // tile_width), axis=1)
        divisor = vir_ref[pl.ds(b, 1), :] - occ
        value = (ladder + other_ref[b].astype(jnp.float32)) / divisor
        live = columns < tile_width * tiles_ref[b]
        out_ref[b] = jnp.where(live, value, jnp.zeros_like(value)).astype(out_ref.dtype)

    @pl.loop(1, planes)
    def _(k):
        amp_copy(k).wait_send()

    @pl.loop(0, planes)
    def _(k):
        relay_copy(k).wait_send()

    @pl.loop(1, pair_count)
    def _(i):
        for copy in back_copies(i):
            copy.wait_send()

    @pl.loop(0, pair_count)
    def _(i):
        for e in range(1, slab_count):
            for copy in part_copies(i, e):
                copy.wait_send()


def kernel_path(kernel, capacity, amplitudes, integrals, other_terms, occ_energy, vir_energy, block_tiles, block_irrep, inverse, needed, rank):
    n = lax.axis_size("pair")
    m = lax.axis_size("slab")
    slots, depth, width = integrals.shape
    rows = amplitudes.shape[2]
    share = rows // m
    blocks = n * slots
    turned = jnp.swapaxes(amplitudes, 1, 2)
    occ_wide = jnp.broadcast_to(occ_energy[:, :, None], occ_energy.shape + (tile_width,))
    smem = pl.BlockSpec(memory_space=pltpu.SMEM)
    vmem = pl.BlockSpec(memory_space=pltpu.VMEM)
    f32, i16, bf16 = jnp.float32, jnp.int16, jnp.bfloat16
    return pl.pallas_call(
        functools.partial(kernel, n, m, capacity),
        out_shape=jax.ShapeDtypeStruct(other_terms.shape, bf16),
        in_specs=[smem] * 5 + [vmem, pl.BlockSpec(memory_space=pl.ANY)] + [vmem] * 3,
        out_specs=vmem,
        scratch_shapes=[
            pltpu.VMEM((slots, depth, width), bf16),
            pltpu.VMEM((n, capacity, rows, depth), bf16),
            pltpu.VMEM((n, capacity, rows, depth), bf16),
            pltpu.VMEM((rows, width), f32),
            pltpu.VMEM((n, slots, share, width), f32),
            pltpu.VMEM((n, m - 1, slots, share, width), i16),
            pltpu.VMEM((n, m - 1, slots, width), f32),
            pltpu.VMEM((n, m - 1, slots, share, width), i16),
            pltpu.VMEM((n, m - 1, slots, width), f32),
            pltpu.VMEM((n, slots, share, width), i16),
            pltpu.VMEM((n, slots, width), f32),
            pltpu.VMEM((blocks, share, width), i16),
            pltpu.VMEM((blocks, width), f32),
            pltpu.SemaphoreType.DMA((slots,)),
            pltpu.SemaphoreType.DMA((2, n)),
            pltpu.SemaphoreType.DMA((2, n, m - 1)),
            pltpu.SemaphoreType.DMA((2, n, m - 1)),
            pltpu.SemaphoreType.DMA((2, n)),
            pltpu.SemaphoreType.DMA((2, n)),
        ],
        compiler_params=pltpu.CompilerParams(
            collective_id=capacity, has_side_effects=True, vmem_limit_bytes=50 * 1024 * 1024
        ),
        cost_estimate=pl.CostEstimate(
            flops=2 * slots * n * rows * depth * width, bytes_accessed=2 * slots * depth * width, transcendentals=0
        ),
    )(needed, rank, inverse, block_irrep, block_tiles, turned, integrals, other_terms, occ_wide, vir_energy)


def shards(
    amplitudes,
    integrals,
    other_terms,
    occ_energy,
    vir_energy,
    block_tiles,
    block_irrep,
    block_order,
):
    whole = (amplitudes, integrals, other_terms, occ_energy, vir_energy, block_tiles, block_irrep, block_order)
    n = lax.axis_size("pair")
    slots = integrals.shape[0]
    share = amplitudes.shape[2] // lax.axis_size("slab")
    if share % 16 or slots % 8 or n % 4 or n > 16:
        return gathered_path(*whole)
    numbers = jnp.arange(n * slots, dtype=jnp.int32)
    inverse = jnp.sum(jnp.where(block_order[None, :] == numbers[:, None], numbers[None, :], 0), axis=1)
    labels = jnp.sum(jnp.where(block_order[:, None] == numbers[None, :], block_irrep[None, :], 0), axis=1)

    def ranks(group):
        held = labels.reshape(-1, group)
        changed = (held[:, 1:] != held[:, :-1]).astype(jnp.int32)
        changed = jnp.pad(changed, ((0, 0), (1, 0)))
        order = jnp.arange(group, dtype=jnp.int32)
        upto = order[None, None, :] <= order[None, :, None]
        return jnp.sum(jnp.where(upto, changed[:, None, :], 0), axis=2)

    device_rank, plane_rank = ranks(slots), ranks(2 * slots)

    def run(kernel, capacity, rank):
        group = rank.shape[1]
        places = jnp.arange(capacity, dtype=jnp.int32)
        held = labels.reshape(-1, group)
        needed = jnp.max(jnp.where(rank[:, :, None] == places, held[:, :, None], 0), axis=1)
        needed = jnp.repeat(needed, group // slots, axis=0)
        places_of = rank.reshape(n, slots)
        return lambda: kernel_path(
            kernel, capacity, amplitudes, integrals, other_terms, occ_energy, vir_energy, block_tiles, block_irrep, inverse, needed, places_of
        )

    relayed = jnp.clip(jnp.max(plane_rank) - 1, 1, 4)
    choice = jnp.where(jnp.max(device_rank) < 2, 0, relayed)
    return lax.switch(
        choice,
        [
            run(ladder_kernel, 2, device_rank),
            run(relay_kernel, 3, plane_rank),
            run(relay_kernel, 4, plane_rank),
            run(relay_kernel, 5, plane_rank),
            lambda: gathered_path(*whole),
        ],
    )


def solution(mesh):
    return jax.shard_map(
        shards,
        mesh=mesh,
        in_specs=(
            P(None, "slab", "pair"),
            P("pair", "slab", None),
            P(None, ("pair", "slab"), None),
            P(None, ("pair", "slab")),
            P(),
            P(),
            P(),
            P(),
        ),
        out_specs=P(None, ("pair", "slab"), None),
        check_vma=False,
    )
```
